512 devices in a mesh: dp: 16 (over z_hi, x), expert: 32 (over y, z_lo, core).
Axes of the slice: x: 4, y: 4, z: 16 (z_hi: 4, z_lo: 4; z = z_hi * 4 + z_lo), core: 2. Of those that a mesh axis runs over, the one named last changes fastest.
Arguments:
- tokens: bfloat16 [65536, 1024], P(('dp', 'expert')), may hold values from -6 to 6
- expert_id: int32 [65536, 1], P(('dp', 'expert')), may hold values from 0 to 31; in each aligned block of 128 rows (0 to 127, 128 to 255, ...) at most 8 rows name the same one
- gate_prob: bfloat16 [65536], P(('dp', 'expert')), may hold values from 0.29882812 to 1
- w_in: bfloat16 [32, 1024, 4096], P('expert', None, 'dp'), may hold values from -0.1875 to 0.1875
- w_out: bfloat16 [32, 4096, 1024], P('expert', 'dp'), may hold values from -0.09375 to 0.09375
- head: bfloat16 [1024, 512], replicated, may hold values from -0.1875 to 0.1875
- image_cache: bfloat16 [4096, 512], P(('dp', 'expert')), may hold values from -25 to 25
- text_cache: bfloat16 [4096, 512], P(('dp', 'expert')), may hold values from -5.1 to 5.1
- pair_label: int32 [4096], P(('dp', 'expert')), may hold values from 0 to 4095, each once
Outputs:
- grad_image: float32 [4096, 512], P(('dp', 'expert'))
- grad_in: float32 [32, 1024, 4096], P('expert', None, 'dp')
- grad_out: float32 [32, 4096, 1024], P('expert', 'dp')
The draws below stay inside these ranges and needn't reach their ends.
Inputs may be any that keep to these rules, and one draw needn't show every extreme that they name: `expert_id`: among the 128 tokens of one device no expert is named more than 8 times, a bound that some block reaches. `pair_label`: each caption index appears once.
All inputs are finite; a program needn't handle non-finite values.
Results may differ from the reference program's by a relative error of at most 0.015.
Values may be sent and summed in bfloat16 or wider, within the bound.
No kernel may reach another device: no remote copies, remote signals or barrier semaphores. Data moves between devices by JAX's collectives and lax.ppermute only.
A program may use at most 64 MiB of HBM per device.

```python
import math
import jax
import jax.numpy as jnp
import numpy as np
from jax import lax

D = 1024
FF = 4096
E = 512
TOK_DEV = 128
PAIRS_DEV = 8
EXPERTS = 32
CAP = 8
TOKENS = 65536
PAIRS = 4096
DEVICES = 512


def base_rows(key):
    return jnp.clip(jax.random.normal(key, (PAIRS, E), jnp.float32), -5.0, 5.0)


def draw_text_cache(key, part):
    base = base_rows(key)
    return base.astype(jnp.bfloat16)


def draw_image_cache(key, part):
    key = jax.random.fold_in(key, 7)
    rows = jnp.clip(jax.random.normal(key, (PAIRS, E), jnp.float32), -5.0, 5.0)
    return rows.astype(jnp.bfloat16)


def levels(key, shape, pieces, least, largest):
    loudness = 1.0
    for position, shards_of in pieces:
        heights = jax.random.uniform(jax.random.fold_in(jax.random.fold_in(key, 6), position), (shards_of,), jnp.float32, least / len(pieces), largest / len(pieces))
        loudness = loudness * jnp.repeat(jnp.exp(heights), shape[position] // shards_of).reshape((-1,) + (1,) * (len(shape) - 1 - position))
    return loudness


def assign_block(own_key, own, number, rows, number_of, top, reach, lean):
    order = jax.random.permutation(own_key, number_of)
    crowded, ordinary = shares(number_of, rows * top, reach, lean, True), shares(number_of, rows * top, reach, lean, False)
    places = jnp.arange(number_of)

    def named(lengths, rotation):
        used = int((lengths > 0).sum())
        fixed = max(1, used // 4)
        passed = fixed + (places - fixed + rotation * (used - fixed)) % max(1, number_of - fixed)
        return jnp.zeros((number_of,), jnp.int32).at[order[jnp.where(places < fixed, places, passed)]].set(jnp.asarray(lengths, jnp.int32))

    lengths = jnp.where(number % 4 == 0, named(crowded, number // 4), named(ordinary, number - number // 4 - 1))
    mixed = jax.random.permutation(jax.random.fold_in(own, 3), number_of)
    giver, sink = mixed[0:number_of // 2 * 2:2], mixed[1:number_of // 2 * 2:2]
    margin = jnp.minimum(lengths[giver] - 1, reach - lengths[sink]) // 2
    margin = jnp.where((giver == order[0]) | (sink == order[0]) | (lengths[sink] == 0), 0, jnp.maximum(margin, 0))
    passed = jax.random.randint(jax.random.fold_in(own, 4), (number_of // 2,), 0, 1 << 20) % (margin + 1)
    lengths = lengths.at[giver].add(-passed).at[sink].add(passed)
    labels = jnp.searchsorted(jnp.cumsum(lengths), jnp.arange(rows * top), side="right").astype(jnp.int32)
    listing = labels.reshape(top, rows).T
    listing = listing[jax.random.permutation(jax.random.fold_in(own, 1), rows)]
    rotation = jax.random.randint(jax.random.fold_in(own, 2), (rows, 1), 0, top)
    return jnp.take_along_axis(listing, (jnp.arange(top)[None, :] + rotation) % top, axis=1)


def shares(count, total, reach, skew, full):
    portions = [(1 << 20) // math.isqrt(rank ** skew) + 1 for rank in range(1, count + 1)]
    largest = reach if full else min(reach, max(-(-total // count), total * portions[0] // sum(portions)))
    least = 1 if total - largest >= count - 1 else 0
    given, surplus = [largest] + [least] * (count - 1), total - largest - least * (count - 1)
    while surplus > 0:
        free = [i for i in range(1, count) if given[i] < largest] or [i for i in range(1, count) if given[i] < reach]
        mass, budget = sum([portions[i] for i in free]), surplus
        for i in free:
            more = min(reach - given[i], max(1, budget * portions[i] // mass), surplus)
            given[i] = given[i] + more
            surplus = surplus - more
    return np.array(given)


def normal_values(stream_key, dims, scale, most, pieces=(), held_as=jnp.bfloat16):
    drawn = jax.random.normal(stream_key, dims, jnp.float32) * scale
    if len(pieces) > 0:
        drawn = levels(stream_key, dims, pieces, -0.22, 0.18) * drawn
    return jnp.clip(drawn, min=-most, max=most).astype(held_as)


def setup_inputs(seed: int = 0) -> dict:
    arg_keys = jax.random.split(jax.random.key(seed), 10)
    tokens = normal_values(arg_keys[0], (TOKENS, D), 1.0, 6.0, ((0, 512),))
    expert_id_keys = jax.random.split(jax.random.fold_in(arg_keys[1], 1), TOKENS // TOK_DEV)
    expert_id_turns = jax.random.permutation(jax.random.fold_in(arg_keys[1], 3), TOKENS // TOK_DEV)
    expert_id = jax.vmap(lambda own, number: assign_block(jax.random.fold_in(arg_keys[1], 2), own, number, TOK_DEV, EXPERTS, 1, CAP, 2))(expert_id_keys, expert_id_turns).reshape((TOKENS, 1))
    gate_prob = jnp.clip(0.29882812 + 0.7011719 * jax.random.uniform(arg_keys[2], (TOKENS,), jnp.float32) ** levels(arg_keys[2], (TOKENS,), ((0, 512),), -0.2, 0.2), 0.29882812, 1.0).astype(jnp.bfloat16)
    w_in = normal_values(arg_keys[3], (EXPERTS, D, FF), D ** -0.5, 0.1875, ((0, 32), (2, 16)))
    w_out = normal_values(arg_keys[4], (EXPERTS, FF, D), FF ** -0.5, 0.09375, ((0, 32), (1, 16)))
    head = normal_values(arg_keys[5], (D, E), D ** -0.5, 0.1875)
    image_cache = draw_image_cache(jax.random.fold_in(arg_keys[9], 71), 0)
    text_cache = draw_text_cache(jax.random.fold_in(arg_keys[9], 71), 0)
    pair_label = jax.random.permutation(arg_keys[8], PAIRS).astype(jnp.int32)
    return {"tokens": tokens, "expert_id": expert_id, "gate_prob": gate_prob, "w_in": w_in, "w_out": w_out, "head": head, "image_cache": image_cache, "text_cache": text_cache, "pair_label": pair_label}


LOGIT_SCALE = 0.125
GELU_K = 0.7978845608
GELU_C = 0.044715


def gelu_parts(pre):
    inner = GELU_K * (pre + GELU_C * pre * pre * pre)
    tangent = jnp.tanh(inner)
    value = 0.5 * pre * (1.0 + tangent)
    slope = 0.5 * (1.0 + tangent) + 0.5 * pre * (1.0 - tangent * tangent) * GELU_K * (1.0 + 3.0 * GELU_C * pre * pre)
    return value, slope


def reference(tokens, expert_id, gate_prob, w_in, w_out, head, image_cache, text_cache, pair_label):
    logits = LOGIT_SCALE * jnp.dot(image_cache, text_cache.T, preferred_element_type=jnp.float32)
    top = jnp.max(logits, axis=1, keepdims=True)
    expo = jnp.exp(logits - top)
    total = jnp.sum(expo, axis=1, keepdims=True)
    weights = expo.astype(jnp.bfloat16)
    mixed = jnp.dot(weights, text_cache, preferred_element_type=jnp.float32) / total
    labelled = text_cache[pair_label].astype(jnp.float32)
    grad_image = LOGIT_SCALE * (mixed - labelled)

    rep_grad = grad_image.reshape(DEVICES, PAIRS_DEV, E)[:, 0, :].astype(jnp.bfloat16)
    cotangent = jnp.dot(rep_grad, head.T, preferred_element_type=jnp.float32).astype(jnp.bfloat16)
    device_of = jnp.arange(TOKENS, dtype=jnp.int32) // TOK_DEV
    out_grad = (gate_prob.astype(jnp.float32)[:, None] * cotangent.astype(jnp.float32)[device_of]).astype(jnp.bfloat16)

    chosen = expert_id[:, 0].astype(jnp.int32)
    onehot = (chosen.reshape(DEVICES, TOK_DEV)[:, :, None] == jnp.arange(EXPERTS, dtype=jnp.int32)[None, None, :]).astype(jnp.float32)
    before = jnp.cumsum(onehot, axis=1) - onehot
    rank = jnp.sum(before * onehot, axis=2).reshape(TOKENS).astype(jnp.int32)
    row = device_of * CAP + rank
    x_buffer = jnp.zeros((EXPERTS, DEVICES * CAP, D), jnp.bfloat16).at[chosen, row].set(tokens)
    g_buffer = jnp.zeros((EXPERTS, DEVICES * CAP, D), jnp.bfloat16).at[chosen, row].set(out_grad)

    def one_expert(packed):
        x_rows, dy_rows, first, second = packed
        pre = jnp.dot(x_rows, first, preferred_element_type=jnp.float32)
        value, slope = gelu_parts(pre)
        hidden = value.astype(jnp.bfloat16)
        back = jnp.dot(dy_rows, second.T, preferred_element_type=jnp.float32)
        hidden_grad = (back * slope).astype(jnp.bfloat16)
        grad_first = jnp.dot(x_rows.T, hidden_grad, preferred_element_type=jnp.float32)
        grad_second = jnp.dot(hidden.T, dy_rows, preferred_element_type=jnp.float32)
        return grad_first, grad_second

    grad_in, grad_out = lax.map(one_expert, (x_buffer, g_buffer, w_in, w_out))
    return grad_image, grad_in, grad_out
```

```python
import jax
import jax.numpy as jnp
from jax import lax
from jax.experimental import pallas as pl
from jax.experimental.pallas import tpu as pltpu
from jax.sharding import PartitionSpec as P

LOGIT_SCALE = 0.125
GELU_K = 0.7978845608
GELU_C = 0.044715
SIDE = 4
HOPS = (0, -1, 1, 2)
BF = jnp.bfloat16
F32 = jnp.float32


def contract(a, b, da, db):
    return lax.dot_general(a, b, (((da,), (db,)), ((), ())), preferred_element_type=F32)


def gelu_parts(pre):
    inner = GELU_K * (pre + GELU_C * pre * pre * pre)
    tangent = jnp.tanh(inner)
    value = 0.5 * pre * (1.0 + tangent)
    slope = 0.5 * (1.0 + tangent) + 0.5 * pre * (1.0 - tangent * tangent) * GELU_K * (
        1.0 + 3.0 * GELU_C * pre * pre
    )
    return (value, slope)


def shift_z(a, by):
    ring = [
        (z * SIDE + x, (z + by) % SIDE * SIDE + x) for z in range(SIDE) for x in range(SIDE)
    ]
    return lax.ppermute(a, "dp", ring)


def shift_x(a, by):
    ring = [
        (z * SIDE + x, z * SIDE + (x + by) % SIDE) for z in range(SIDE) for x in range(SIDE)
    ]
    return lax.ppermute(a, "dp", ring)


def gather_z(own):
    half = own.shape[0] // 2
    before, after = shift_z(own, 1), shift_z(own, -1)
    far = [shift_z(before[:half], 1), shift_z(after[half:], -1)]
    return [own, before, after, jnp.concatenate(far, axis=0)]


def gather_x(own, way):
    before, after = shift_x(own, 1), shift_x(own, -1)
    far = shift_x(before, 1) if way > 0 else shift_x(after, -1)
    return [own, before, after, far]


def expert_kernel(*refs):
    n = SIDE * SIDE
    x_refs = refs[:n]
    first_ref, back_hi_ref, back_lo_ref, gate_ref, cot_ref, grad_in_ref, grad_out_ref, acc, sums = refs[n:]
    rows = x_refs[0].shape[0]
    images = sums.shape[0] // n
    per = rows // images
    first = first_ref[...]
    mask = (
        lax.broadcasted_iota(jnp.int32, (images, rows), 1) // per
        == lax.broadcasted_iota(jnp.int32, (images, rows), 0)
    )
    for c in range(n):
        here = pl.ds(c * images, images)
        x = x_refs[c][...]
        spread = jnp.where(mask, gate_ref[c : c + 1, :].astype(F32), 0.0).astype(BF)
        pre = jnp.dot(x, first, preferred_element_type=F32)
        value, slope = gelu_parts(pre)
        hidden = value.astype(BF)
        back = contract(spread, back_hi_ref[here, :], 0, 0) + contract(
            spread, back_lo_ref[here, :], 0, 0
        )
        hidden_grad = (back * slope).astype(BF)
        term = contract(hidden_grad, x, 0, 0)
        if c == 0:
            acc[...] = term
        else:
            acc[...] += term
        sums[here, :] = jnp.dot(spread, hidden, preferred_element_type=F32).astype(BF)
    grad_in_ref[...] = acc[...].T
    grad_out_ref[...] = contract(sums[...], cot_ref[...], 0, 0)


def expert_grads(pieces, first, back_hi, back_lo, gates, cot):
    rows, width = pieces[0].shape
    hidden = first.shape[1]
    vmem = pl.BlockSpec(memory_space=pltpu.VMEM)
    return pl.pallas_call(
        expert_kernel,
        out_shape=(
            jax.ShapeDtypeStruct((width, hidden), F32),
            jax.ShapeDtypeStruct((hidden, width), F32),
        ),
        in_specs=[vmem] * (len(pieces) + 5),
        out_specs=(vmem, vmem),
        scratch_shapes=[
            pltpu.VMEM((hidden, width), F32),
            pltpu.VMEM((cot.shape[0], hidden), BF),
        ],
        compiler_params=pltpu.CompilerParams(vmem_limit_bytes=32 * 1024 * 1024),
        cost_estimate=pl.CostEstimate(
            flops=5_000_000_000, bytes_accessed=13_000_000, transcendentals=1_000_000
        ),
    )(*pieces, first, back_hi, back_lo, gates, cot)


def body(tokens, expert_id, gate_prob, w_in, w_out, head, image_cache, text_cache, pair_label):
    n_tok, width = tokens.shape
    n_exp = lax.axis_size("expert")
    n_dp = lax.axis_size("dp")
    capacity = 2 * n_tok // n_exp
    n_slots = n_exp * capacity
    n_pairs, wide = image_cache.shape
    row = lax.axis_index("dp")
    first = w_in[0]
    second = w_out[0]

    label_parts = jnp.stack([pair_label // 64, pair_label % 64], axis=1).astype(BF)
    label_parts = jnp.pad(label_parts, ((0, 0), (0, 126)))
    column = lax.all_gather(
        jnp.concatenate([image_cache, label_parts], axis=1), "dp", axis=0, tiled=True
    )

    chosen = expert_id[:, 0]
    onehot = (chosen[:, None] == jnp.arange(n_exp, dtype=jnp.int32)[None, :]).astype(BF)
    lower = (jnp.arange(n_tok)[:, None] > jnp.arange(n_tok)[None, :]).astype(BF)
    before = jnp.dot(lower, onehot, preferred_element_type=F32)
    rank = jnp.sum(before * onehot.astype(F32), axis=1).astype(jnp.int32)
    position = chosen * capacity + rank
    dispatch = (position[:, None] == jnp.arange(n_slots, dtype=jnp.int32)[None, :]).astype(BF)
    x_buffer = contract(dispatch, tokens, 0, 0).astype(BF).reshape(n_exp, capacity, width)
    slot_gate = contract(dispatch, jnp.broadcast_to(gate_prob[:, None], (n_tok, 128)), 0, 0)
    slot_gate = slot_gate.astype(BF).reshape(n_exp, capacity, 128)
    captions = jnp.broadcast_to(text_cache[None], (n_exp, n_pairs, wide))
    sent = jnp.concatenate([x_buffer, captions, slot_gate], axis=2)
    got = lax.all_to_all(sent, "expert", split_axis=0, concat_axis=0, tiled=True)
    own = got[:, :, :width].reshape(n_slots, width)
    block = got[:, :, width : width + wide].reshape(n_exp * n_pairs, wide)
    gate_col = got[:, :, width + wide :].reshape(n_slots, 128)
    eye = (jnp.arange(n_slots)[:, None] == jnp.arange(n_slots)[None, :]).astype(F32)
    gate_row = jnp.sum(eye * gate_col[:, :1].astype(F32), axis=0, keepdims=True).astype(BF)

    pieces = []
    for i, piece in enumerate(gather_z(own)):
        pieces += gather_x(piece, 1 if i % 2 == 0 else -1)

    images = column[:, :wide]
    labels = column[:, wide].astype(jnp.int32) * 64 + column[:, wide + 1].astype(jnp.int32)
    logits = LOGIT_SCALE * contract(images, block, 1, 1)
    top = lax.reduce_precision(jnp.max(logits, axis=1, keepdims=True), 8, 7)
    expo = jnp.exp(logits - top)
    total = jnp.sum(expo, axis=1, keepdims=True)
    mix = jnp.dot(expo.astype(BF), block, preferred_element_type=F32)
    ids = row * block.shape[0] + jnp.arange(block.shape[0], dtype=jnp.int32)
    hits = (labels[:, None] == ids[None, :]).astype(BF)
    labelled = jnp.dot(hits, block, preferred_element_type=F32)
    total_hi = lax.reduce_precision(total, 8, 7)
    stats = jnp.concatenate([top, total_hi, total - total_hi], axis=1)
    stats = jnp.pad(stats, ((0, 0), (0, 125))).astype(BF)
    gates_out = jnp.broadcast_to(gate_row, (n_dp * n_pairs, n_slots))
    part = jnp.concatenate([mix.astype(BF), labelled.astype(BF), gates_out, stats], axis=1)
    part = part.reshape(n_dp, n_pairs, part.shape[1])
    part = lax.all_to_all(part, "dp", split_axis=0, concat_axis=0, tiled=True)
    stats = part[:, :, 2 * wide + n_slots :].astype(F32)
    tops = stats[:, :, 0:1]
    scale = jnp.exp(tops - jnp.max(tops, axis=0, keepdims=True))
    total = jnp.sum((stats[:, :, 1:2] + stats[:, :, 2:3]) * scale, axis=0)
    mixed = jnp.sum(part[:, :, :wide].astype(F32) * scale, axis=0) / total
    labelled = jnp.sum(part[:, :, wide : 2 * wide].astype(F32), axis=0)
    grad_image = LOGIT_SCALE * (mixed - labelled)
    rep_grad = grad_image[:1].astype(BF)

    z_hi, x = row // SIDE, row % SIDE
    order = jnp.stack(
        [(z_hi + i) % SIDE * SIDE + (x + j) % SIDE for i in HOPS for j in HOPS]
    )
    pick = (order[:, None] == jnp.arange(n_dp, dtype=jnp.int32)[None, :]).astype(BF)
    gates = jnp.dot(pick, part[:, 0, 2 * wide : 2 * wide + n_slots], preferred_element_type=F32)
    reps = lax.all_to_all(
        jnp.broadcast_to(rep_grad[None], (n_dp, 1, wide)), "dp", split_axis=0, concat_axis=0, tiled=True
    )
    reps = jnp.dot(pick, reps[:, 0], preferred_element_type=F32).astype(BF)
    reps = lax.all_to_all(
        jnp.broadcast_to(reps[None], (n_exp, n_dp, wide)), "expert", split_axis=0, concat_axis=0, tiled=True
    )
    reps = jnp.transpose(reps, (1, 0, 2)).reshape(n_dp * n_exp, wide)
    cot = contract(reps, head, 1, 1).astype(BF)
    back = contract(cot, second, 1, 1)
    back_hi = lax.reduce_precision(back, 8, 7)
    grad_in, grad_out = expert_grads(
        pieces, first, back_hi.astype(BF), (back - back_hi).astype(BF), gates.astype(BF), cot
    )
    return (grad_image, grad_in[None], grad_out[None])


def solution(mesh):
    placed = (
        P(("dp", "expert"), None),
        P(("dp", "expert"), None),
        P(("dp", "expert")),
        P("expert", None, "dp"),
        P("expert", "dp", None),
        P(),
        P(("dp", "expert"), None),
        P(("dp", "expert"), None),
        P(("dp", "expert")),
    )
    return jax.shard_map(
        body,
        mesh=mesh,
        in_specs=placed,
        out_specs=(P(("dp", "expert"), None), P("expert", None, "dp"), P("expert", "dp", None)),
        check_vma=False,
    )
```

```python
import jax
import jax.numpy as jnp
import numpy as np
from jax import lax
from jax.experimental import pallas as pl
from jax.experimental.pallas import tpu as pltpu
from jax.sharding import PartitionSpec as P

LOGIT_SCALE = 0.125
GELU_K = 0.7978845608
GELU_C = 0.044715
SIDE = 4
SIDES = {
    "z_hi": ("dp", (SIDE, SIDE), 0),
    "x": ("dp", (SIDE, SIDE), 1),
    "y": ("expert", (SIDE, SIDE, 2), 0),
    "z_lo": ("expert", (SIDE, SIDE, 2), 1),
    "core": ("expert", (SIDE, SIDE, 2), 2),
}
BF = jnp.bfloat16
F32 = jnp.float32


def contract(a, b, da, db):
    return lax.dot_general(a, b, (((da,), (db,)), ((), ())), preferred_element_type=F32)


def gelu_parts(pre):
    inner = GELU_K * (pre + GELU_C * pre * pre * pre)
    tangent = jnp.tanh(inner)
    value = 0.5 * pre * (1.0 + tangent)
    slope = 0.5 * (1.0 + tangent) + 0.5 * pre * (1.0 - tangent * tangent) * GELU_K * (
        1.0 + 3.0 * GELU_C * pre * pre
    )
    return (value, slope)


def shift(a, axis, by):
    name, sizes, side = SIDES[axis]
    ring = []
    for at in np.ndindex(*sizes):
        to = list(at)
        to[side] = (to[side] + by) % sizes[side]
        ring.append((int(np.ravel_multi_index(at, sizes)), int(np.ravel_multi_index(to, sizes))))
    return lax.ppermute(a, name, ring)


def spread_along(a, axis):
    name, sizes, side = SIDES[axis]
    return [a] + [shift(a, axis, k) for k in range(1, sizes[side])]


def gather_x(a):
    rows = [[z * SIDE + x for x in range(SIDE)] for z in range(SIDE)]
    return lax.all_gather(a, "dp", axis=0, tiled=True, axis_index_groups=rows)


def after(a, *others):
    return lax.optimization_barrier((a, *others))[0]


def loss_kernel(*refs):
    n = 4 * SIDE // 2
    parts = refs[:n]
    want_ref, image_ref, own_meta_ref, head_ref, second_ref = refs[n : n + 5]
    grad_image_ref, cot_ref, back_hi_ref, back_lo_ref, gate_ref = refs[n + 5 : n + 10]
    images, reps, metas, logit, weights, hits = refs[n + 10 :]
    n_rep = want_ref.shape[0]
    n_own = image_ref.shape[0]
    n_all = images.shape[0]
    each = n_rep // n // SIDE
    step = n_own * each * SIDE
    block = (n_own + 2) * each
    row, expert = lax.axis_index("dp"), lax.axis_index("expert")
    z_hi, x = row >> 2, row & 3
    y, z_lo, core = expert >> 3, expert >> 1 & 3, expert & 1

    def device(part, k):
        at = ((z_hi - (k & 3)) & 3) * 4 + ((x - (k >> 4)) & 3)
        at = (at * 4 + ((y - part % SIDE) & 3)) * 4 + ((z_lo - (k >> 2 & 3)) & 3)
        return at * 2 + ((core - part // SIDE) & 1)

    def counted(size):
        return lax.broadcasted_iota(jnp.int32, (1, size), 1)

    def gathered(offset):
        for p, ref in enumerate(parts):
            for q in range(SIDE):
                to = (p * SIDE + q) * each
                reps[pl.ds(to, each), :] = ref[pl.ds(q * block + offset, each), :]
        return reps[...]

    def captions(ref):
        return jnp.concatenate([ref[pl.ds(q * block, n_own * each), :] for q in range(SIDE)], axis=0)

    sources = jnp.concatenate([device(p, counted(SIDE * each)) for p in range(n)], axis=1)
    pick = (want_ref[...] == sources).astype(BF)
    images[:n_rep, :] = jnp.dot(pick, gathered(n_own * each), preferred_element_type=F32).astype(BF)
    images[n_rep:, :] = jnp.zeros((n_all - n_rep, images.shape[1]), BF)
    images[n_rep : n_rep + n_own, :] = image_ref[...]
    found = jnp.dot(pick, gathered((n_own + 1) * each), preferred_element_type=F32)
    width = found.shape[1]
    source = lax.broadcasted_iota(jnp.int32, (width, 128), 0)
    slot = lax.broadcasted_iota(jnp.int32, (width, 128), 1)
    label_at = 256
    select = jnp.where(slot < 8, expert * 8 + slot, label_at + slot - 8)
    select = ((source == select) & (slot < 10)).astype(BF)
    found = jnp.dot(found.astype(BF), select, preferred_element_type=F32)
    gate_ref[...] = found.astype(BF)
    metas[:n_rep, :] = found
    metas[n_rep:, :] = jnp.full((n_all - n_rep, 128), -8.0, F32)
    metas[n_rep : n_rep + n_own, :] = own_meta_ref[...]
    labels = (metas[:, 8:9] * 64.0 + metas[:, 9:10]).astype(jnp.int32)
    top = None
    for p, ref in enumerate(parts):
        ids = device(p, counted(step) >> 3) * 8 + (counted(step) & 7)
        part = LOGIT_SCALE * contract(images[...], captions(ref), 1, 1)
        logit[:, pl.ds(p * step, step)] = part
        hits[:, pl.ds(p * step, step)] = (labels == ids).astype(BF)
        peak = jnp.max(part, axis=1, keepdims=True)
        top = peak if top is None else jnp.maximum(top, peak)
    total = jnp.zeros((n_all, 1), F32)
    for p in range(n):
        expo = jnp.exp(logit[:, pl.ds(p * step, step)] - top)
        total = total + jnp.sum(expo, axis=1, keepdims=True)
        weights[:, pl.ds(p * step, step)] = expo.astype(BF)
    mix, labelled = jnp.zeros(images.shape, F32), jnp.zeros(images.shape, F32)
    for p, ref in enumerate(parts):
        rows = captions(ref)
        mix += jnp.dot(weights[:, pl.ds(p * step, step)], rows, preferred_element_type=F32)
        labelled += jnp.dot(hits[:, pl.ds(p * step, step)], rows, preferred_element_type=F32)
    grad = LOGIT_SCALE * (mix / total - labelled)
    grad_image_ref[...] = grad[n_rep : n_rep + n_own, :]
    cot = contract(grad[:n_rep].astype(BF), head_ref[...], 1, 1).astype(BF)
    cot_ref[...] = cot
    back = contract(cot, second_ref[...], 1, 1)
    back_hi = back.astype(BF)
    back_hi_ref[...] = back_hi
    back_lo_ref[...] = (back - back_hi.astype(F32)).astype(BF)


def image_grads(parts, want, image_cache, own_meta, head, second):
    n_rep, n_own, wide = want.shape[0], image_cache.shape[0], image_cache.shape[1]
    n_all = n_rep + 16
    n_text = n_rep * n_own
    hidden, width = second.shape
    vmem = pl.BlockSpec(memory_space=pltpu.VMEM)
    return pl.pallas_call(
        loss_kernel,
        out_shape=(
            jax.ShapeDtypeStruct((n_own, wide), F32),
            jax.ShapeDtypeStruct((n_rep, width), BF),
            jax.ShapeDtypeStruct((n_rep, hidden), BF),
            jax.ShapeDtypeStruct((n_rep, hidden), BF),
            jax.ShapeDtypeStruct((n_rep, 128), BF),
        ),
        in_specs=[vmem] * (len(parts) + 5),
        out_specs=(vmem,) * 5,
        scratch_shapes=[
            pltpu.VMEM((n_all, wide), BF),
            pltpu.VMEM((n_rep, wide), BF),
            pltpu.VMEM((n_all, 128), F32),
            pltpu.VMEM((n_all, n_text), F32),
            pltpu.VMEM((n_all, n_text), BF),
            pltpu.VMEM((n_all, n_text), BF),
        ],
        compiler_params=pltpu.CompilerParams(vmem_limit_bytes=60 * 1024 * 1024),
        cost_estimate=pl.CostEstimate(
            flops=10_000_000_000, bytes_accessed=9_000_000, transcendentals=3_000_000
        ),
    )(*parts, want, image_cache, own_meta, head, second)


def expert_kernel(*refs):
    n = len(refs) - 16
    sources, targets = refs[: n + 5], refs[n + 7 : n + 12]
    grad_in_ref, grad_out_ref = refs[n + 5 : n + 7]
    acc, sums, held = refs[n + 12 : n + 15]
    sems = refs[n + 15]
    first_ref, back_hi_ref, back_lo_ref, gate_ref, cot_ref = targets
    copies, at = [], 0
    for i in range(5):
        copies.append(pltpu.make_async_copy(sources[n + i], targets[i], sems.at[n + i]))
    for i in range(n):
        size = sources[i].shape[0]
        copies.append(pltpu.make_async_copy(sources[i], held.at[pl.ds(at, size)], sems.at[i]))
        at += size
    for copy in copies[:4] + copies[5:] + copies[4:5]:
        copy.start()
    for copy in copies[:4]:
        copy.wait()
    images = 32
    per = 8
    rows = images * per
    first = first_ref[...]
    column = lax.broadcasted_iota(jnp.int32, (images, rows), 1)
    mask = column // per == lax.broadcasted_iota(jnp.int32, (images, rows), 0)
    widen = (
        lax.broadcasted_iota(jnp.int32, (128, rows), 1) % per
        == lax.broadcasted_iota(jnp.int32, (128, rows), 0)
    ).astype(BF)
    c = 0
    for i in range(n):
        copies[5 + i].wait()
        for _ in range(sources[i].shape[0] // rows):
            here = pl.ds(c * images, images)
            x = held[pl.ds(c * rows, rows), :]
            gates = jnp.dot(gate_ref[here, :], widen, preferred_element_type=F32)
            spread = jnp.where(mask, gates, 0.0).astype(BF)
            pre = jnp.dot(x, first, preferred_element_type=F32)
            value, slope = gelu_parts(pre)
            hidden = value.astype(BF)
            back = contract(spread, back_hi_ref[here, :], 0, 0) + contract(
                spread, back_lo_ref[here, :], 0, 0
            )
            hidden_grad = (back * slope).astype(BF)
            term = contract(hidden_grad, x, 0, 0)
            if c == 0:
                acc[...] = term
            else:
                acc[...] += term
            sums[here, :] = jnp.dot(spread, hidden, preferred_element_type=F32).astype(BF)
            c += 1
    copies[4].wait()
    grad_in_ref[...] = acc[...].T
    grad_out_ref[...] = contract(sums[...], cot_ref[...], 0, 0)


def expert_grads(pieces, first, back_hi, back_lo, gates, cot):
    width, hidden = first.shape
    vmem = pl.BlockSpec(memory_space=pltpu.VMEM)
    rest = (first, back_hi, back_lo, gates, cot)
    return pl.pallas_call(
        expert_kernel,
        out_shape=(
            jax.ShapeDtypeStruct((width, hidden), F32),
            jax.ShapeDtypeStruct((hidden, width), F32),
        ),
        in_specs=[pl.BlockSpec(memory_space=pltpu.HBM)] * (len(pieces) + 5),
        out_specs=(vmem, vmem),
        scratch_shapes=[
            *(pltpu.VMEM(r.shape, BF) for r in rest),
            pltpu.VMEM((hidden, width), F32),
            pltpu.VMEM((cot.shape[0], hidden), BF),
            pltpu.VMEM((sum(p.shape[0] for p in pieces), width), BF),
            pltpu.SemaphoreType.DMA((len(pieces) + 5,)),
        ],
        compiler_params=pltpu.CompilerParams(vmem_limit_bytes=60 * 1024 * 1024),
        cost_estimate=pl.CostEstimate(
            flops=5_000_000_000, bytes_accessed=13_000_000, transcendentals=1_000_000
        ),
    )(*pieces, *rest)


def slots(chosen, n_exp, capacity):
    n_tok = chosen.shape[0]
    onehot = (chosen[:, None] == jnp.arange(n_exp, dtype=jnp.int32)[None, :]).astype(BF)
    lower = (jnp.arange(n_tok)[:, None] > jnp.arange(n_tok)[None, :]).astype(BF)
    before = jnp.dot(lower, onehot, preferred_element_type=F32)
    rank = jnp.sum(before * onehot.astype(F32), axis=1).astype(jnp.int32)
    position = chosen * capacity + rank
    return (position[:, None] == jnp.arange(n_exp * capacity, dtype=jnp.int32)[None, :]).astype(BF)


def body(tokens, expert_id, gate_prob, w_in, w_out, head, image_cache, text_cache, pair_label):
    n_tok, width = tokens.shape
    n_exp = lax.axis_size("expert")
    n_dp = lax.axis_size("dp")
    capacity = 2 * n_tok // n_exp
    n_slots = n_exp * capacity
    n_pairs, wide = image_cache.shape
    row = lax.axis_index("dp")
    z_hi, x = row // SIDE, row % SIDE
    first = w_in[0]
    second = w_out[0]

    chosen = expert_id[:, :1]

    dispatch = slots(chosen[:, 0], n_exp, capacity)
    buffer = contract(dispatch, tokens, 0, 0).astype(BF).reshape(n_exp, capacity, width)
    own = lax.all_to_all(buffer, "expert", split_axis=0, concat_axis=0, tiled=True)
    own = own.reshape(n_slots, width)

    label_parts = jnp.stack([pair_label // 64, pair_label % 64], axis=1).astype(BF)
    slot_gate = jnp.dot(gate_prob[None, :], dispatch, preferred_element_type=F32).astype(BF)
    meta = jnp.concatenate([slot_gate, label_parts[:1], jnp.zeros((1, wide - n_slots - 2), BF)], axis=1)
    known = jnp.concatenate([text_cache, image_cache[:1], meta, jnp.zeros((6, wide), BF)], axis=0)
    known = jnp.stack(spread_along(known, "z_hi"))
    cuts = (0, n_pairs, n_pairs + 1, n_pairs + 2)
    known = [known[:, i:j].reshape(-1, wide) for i, j in zip(cuts, cuts[1:])]
    known = jnp.concatenate(known, axis=0)
    own = after(own, known)
    got = jnp.stack(spread_along(known, "z_lo"))
    cuts = tuple(SIDE * c for c in cuts)
    known = [got[:, i:j].reshape(-1, wide) for i, j in zip(cuts, cuts[1:])]
    known = jnp.concatenate(known, axis=0)

    later = after(own, known)
    below, above = shift(later, "z_hi", 1), shift(later, "z_hi", -1)
    known = spread_along(known, "x")
    near = spread_along(jnp.concatenate(known, axis=0), "y")

    own_x = gather_x(own)
    below, above = after(below, *near[1:]), after(above, *near[1:])
    half = n_slots // 2
    far = jnp.concatenate([shift(below[:half], "z_hi", 1), shift(above[half:], "z_hi", -1)], axis=0)
    both = jnp.concatenate([below, above], axis=0)
    left, right = shift(both, "x", 1), shift(both, "x", -1)
    left_far, right_far = shift(left[:n_slots], "x", 1), shift(right[n_slots:], "x", -1)
    far = after(far, left, right)
    far = [far, shift(far, "x", 1), shift(far, "x", -1), shift(far, "x", 2)]
    pieces = [own_x, both, left, right, left_far, right_far] + far
    other = [shift(p, "core", 1) for p in near]

    places = [(0, j, 0) for j in range(SIDE)]
    places += [(i, j, 1) for j in (0, -1, 1, 2) for i in (-1, 1)]
    places += [(2, j, 1) for j in (0, -1, 1, 2)]
    along_z, along_x, moved = (jnp.asarray(c, jnp.int32) for c in np.asarray(places).T)
    order = (z_hi + along_z) % SIDE * SIDE + (x * moved + along_x) % SIDE
    want = (order[:, None] * n_exp + jnp.arange(n_exp, dtype=jnp.int32)[None, :]).reshape(-1, 1)
    own_meta = jnp.pad(label_parts.astype(F32), ((0, 0), (8, 118)))

    grad_image, cot, back_hi, back_lo, gates = image_grads(
        [after(near[0], left, right)] + near[1:] + other, want, image_cache, own_meta, head, second
    )
    grad_in, grad_out = expert_grads(pieces, first, back_hi, back_lo, gates, cot)
    return (grad_image, grad_in[None], grad_out[None])


def solution(mesh):
    placed = (
        P(("dp", "expert"), None),
        P(("dp", "expert"), None),
        P(("dp", "expert")),
        P("expert", None, "dp"),
        P("expert", "dp", None),
        P(),
        P(("dp", "expert"), None),
        P(("dp", "expert"), None),
        P(("dp", "expert")),
    )
    return jax.shard_map(
        body,
        mesh=mesh,
        in_specs=placed,
        out_specs=(P(("dp", "expert"), None), P("expert", None, "dp"), P("expert", "dp", None)),
        check_vma=False,
    )
```

```python
import jax
import jax.numpy as jnp
import numpy as np
from jax import lax
from jax.experimental import pallas as pl
from jax.experimental.pallas import tpu as pltpu
from jax.sharding import PartitionSpec as P

LOGIT_SCALE = 0.125
GELU_K = 0.7978845608
GELU_C = 0.044715
SIDE = 4
SIDES = {
    "z_hi": ("dp", (SIDE, SIDE), 0),
    "x": ("dp", (SIDE, SIDE), 1),
    "y": ("expert", (SIDE, SIDE, 2), 0),
    "z_lo": ("expert", (SIDE, SIDE, 2), 1),
    "core": ("expert", (SIDE, SIDE, 2), 2),
}
BF = jnp.bfloat16
F32 = jnp.float32


def contract(a, b, da, db):
    return lax.dot_general(a, b, (((da,), (db,)), ((), ())), preferred_element_type=F32)


def gelu_parts(pre):
    inner = GELU_K * (pre + GELU_C * pre * pre * pre)
    tangent = jnp.tanh(inner)
    value = 0.5 * pre * (1.0 + tangent)
    slope = 0.5 * (1.0 + tangent) + 0.5 * pre * (1.0 - tangent * tangent) * GELU_K * (
        1.0 + 3.0 * GELU_C * pre * pre
    )
    return (value, slope)


def shift(a, axis, by):
    name, sizes, side = SIDES[axis]
    ring = []
    for at in np.ndindex(*sizes):
        to = list(at)
        to[side] = (to[side] + by) % sizes[side]
        ring.append((int(np.ravel_multi_index(at, sizes)), int(np.ravel_multi_index(to, sizes))))
    return lax.ppermute(a, name, ring)


def spread_along(a, axis):
    name, sizes, side = SIDES[axis]
    return [a] + [shift(a, axis, k) for k in range(1, sizes[side])]


def gather_x(a):
    rows = [[z * SIDE + x for x in range(SIDE)] for z in range(SIDE)]
    return lax.all_gather(a, "dp", axis=0, tiled=True, axis_index_groups=rows)


def after(a, *others):
    return lax.optimization_barrier((a, *others))[0]


def loss_kernel(*refs):
    n = 4 * SIDE // 2
    halves, wholes, refs = refs[:n], refs[n : n + n // 2], refs[n + n // 2 :]
    want_ref, image_ref, own_meta_ref, head_ref, second_ref = refs[:5]
    grad_image_ref, cot_ref, back_hi_ref, back_lo_ref, gate_ref = refs[5:10]
    images, reps, metas, logit, weights, hits = refs[10:]
    n_rep = want_ref.shape[0]
    n_own = image_ref.shape[0]
    n_all = images.shape[0]
    each = n_rep // n // SIDE
    step = n_own * each * SIDE
    block = (n_own + 2) * each
    row, expert = lax.axis_index("dp"), lax.axis_index("expert")
    z_hi, x = row >> 2, row & 3
    y, z_lo, core = expert >> 3, expert >> 1 & 3, expert & 1

    def device(part, k):
        at = ((z_hi - (k & 3)) & 3) * 4 + ((x - (k >> 4)) & 3)
        at = (at * 4 + ((y - part % SIDE) & 3)) * 4 + ((z_lo - (k >> 2 & 3)) & 3)
        return at * 2 + ((core - part // SIDE) & 1)

    def counted(size):
        return lax.broadcasted_iota(jnp.int32, (1, size), 1)

    def piece(p, q, offset, size):
        if p < n // 2:
            return halves[2 * p + q // 2][pl.ds(q % 2 * block + offset, size), :]
        return wholes[p - n // 2][pl.ds(q * block + offset, size), :]

    def gathered(offset):
        for p in range(n):
            for q in range(SIDE):
                reps[pl.ds((p * SIDE + q) * each, each), :] = piece(p, q, offset, each)
        return reps[...]

    def captions(p):
        return jnp.concatenate([piece(p, q, 0, n_own * each) for q in range(SIDE)], axis=0)

    sources = jnp.concatenate([device(p, counted(SIDE * each)) for p in range(n)], axis=1)
    pick = (want_ref[...] == sources).astype(BF)
    images[:n_rep, :] = jnp.dot(pick, gathered(n_own * each), preferred_element_type=F32).astype(BF)
    images[n_rep:, :] = jnp.zeros((n_all - n_rep, images.shape[1]), BF)
    images[n_rep : n_rep + n_own, :] = image_ref[...]
    found = jnp.dot(pick, gathered((n_own + 1) * each), preferred_element_type=F32)
    width = found.shape[1]
    source = lax.broadcasted_iota(jnp.int32, (width, 128), 0)
    slot = lax.broadcasted_iota(jnp.int32, (width, 128), 1)
    label_at = 256
    select = jnp.where(slot < 8, expert * 8 + slot, label_at + slot - 8)
    select = ((source == select) & (slot < 10)).astype(BF)
    found = jnp.dot(found.astype(BF), select, preferred_element_type=F32)
    gate_ref[...] = found.astype(BF)
    metas[:n_rep, :] = found
    metas[n_rep:, :] = jnp.full((n_all - n_rep, 128), -8.0, F32)
    metas[n_rep : n_rep + n_own, :] = own_meta_ref[...]
    labels = (metas[:, 8:9] * 64.0 + metas[:, 9:10]).astype(jnp.int32)
    top = None
    for p in range(n):
        ids = device(p, counted(step) >> 3) * 8 + (counted(step) & 7)
        part = LOGIT_SCALE * contract(images[...], captions(p), 1, 1)
        logit[:, pl.ds(p * step, step)] = part
        hits[:, pl.ds(p * step, step)] = (labels == ids).astype(BF)
        peak = jnp.max(part, axis=1, keepdims=True)
        top = peak if top is None else jnp.maximum(top, peak)
    total = jnp.zeros((n_all, 1), F32)
    for p in range(n):
        expo = jnp.exp(logit[:, pl.ds(p * step, step)] - top)
        total = total + jnp.sum(expo, axis=1, keepdims=True)
        weights[:, pl.ds(p * step, step)] = expo.astype(BF)
    mix, labelled = jnp.zeros(images.shape, F32), jnp.zeros(images.shape, F32)
    for p in range(n):
        rows = captions(p)
        mix += jnp.dot(weights[:, pl.ds(p * step, step)], rows, preferred_element_type=F32)
        labelled += jnp.dot(hits[:, pl.ds(p * step, step)], rows, preferred_element_type=F32)
    grad = LOGIT_SCALE * (mix / total - labelled)
    grad_image_ref[...] = grad[n_rep : n_rep + n_own, :]
    cot = contract(grad[:n_rep].astype(BF), head_ref[...], 1, 1).astype(BF)
    cot_ref[...] = cot
    back = contract(cot, second_ref[...], 1, 1)
    back_hi = back.astype(BF)
    back_hi_ref[...] = back_hi
    back_lo_ref[...] = (back - back_hi.astype(F32)).astype(BF)


def image_grads(parts, want, image_cache, own_meta, head, second):
    n_rep, n_own, wide = want.shape[0], image_cache.shape[0], image_cache.shape[1]
    n_all = n_rep + 16
    n_text = n_rep * n_own
    hidden, width = second.shape
    vmem = pl.BlockSpec(memory_space=pltpu.VMEM)
    return pl.pallas_call(
        loss_kernel,
        out_shape=(
            jax.ShapeDtypeStruct((n_own, wide), F32),
            jax.ShapeDtypeStruct((n_rep, width), BF),
            jax.ShapeDtypeStruct((n_rep, hidden), BF),
            jax.ShapeDtypeStruct((n_rep, hidden), BF),
            jax.ShapeDtypeStruct((n_rep, 128), BF),
        ),
        in_specs=[vmem] * (len(parts) + 5),
        out_specs=(vmem,) * 5,
        scratch_shapes=[
            pltpu.VMEM((n_all, wide), BF),
            pltpu.VMEM((n_rep, wide), BF),
            pltpu.VMEM((n_all, 128), F32),
            pltpu.VMEM((n_all, n_text), F32),
            pltpu.VMEM((n_all, n_text), BF),
            pltpu.VMEM((n_all, n_text), BF),
        ],
        compiler_params=pltpu.CompilerParams(vmem_limit_bytes=60 * 1024 * 1024),
        cost_estimate=pl.CostEstimate(
            flops=10_000_000_000, bytes_accessed=9_000_000, transcendentals=3_000_000
        ),
    )(*parts, want, image_cache, own_meta, head, second)


def expert_kernel(*refs):
    n = len(refs) - 16
    sources, targets = refs[: n + 5], refs[n + 7 : n + 12]
    grad_in_ref, grad_out_ref = refs[n + 5 : n + 7]
    acc, sums, held = refs[n + 12 : n + 15]
    sems = refs[n + 15]
    first_ref, back_hi_ref, back_lo_ref, gate_ref, cot_ref = targets
    copies, at = [], 0
    for i in range(5):
        copies.append(pltpu.make_async_copy(sources[n + i], targets[i], sems.at[n + i]))
    for i in range(n):
        size = sources[i].shape[0]
        copies.append(pltpu.make_async_copy(sources[i], held.at[pl.ds(at, size)], sems.at[i]))
        at += size
    for copy in copies[:4] + copies[5:] + copies[4:5]:
        copy.start()
    for copy in copies[:4]:
        copy.wait()
    images = 32
    per = 8
    rows = images * per
    first = first_ref[...]
    column = lax.broadcasted_iota(jnp.int32, (images, rows), 1)
    mask = column // per == lax.broadcasted_iota(jnp.int32, (images, rows), 0)
    widen = (
        lax.broadcasted_iota(jnp.int32, (128, rows), 1) % per
        == lax.broadcasted_iota(jnp.int32, (128, rows), 0)
    ).astype(BF)
    c = 0
    for i in range(n):
        copies[5 + i].wait()
        for _ in range(sources[i].shape[0] // rows):
            here = pl.ds(c * images, images)
            x = held[pl.ds(c * rows, rows), :]
            gates = jnp.dot(gate_ref[here, :], widen, preferred_element_type=F32)
            spread = jnp.where(mask, gates, 0.0).astype(BF)
            pre = jnp.dot(x, first, preferred_element_type=F32)
            value, slope = gelu_parts(pre)
            hidden = value.astype(BF)
            back = contract(spread, back_hi_ref[here, :], 0, 0) + contract(
                spread, back_lo_ref[here, :], 0, 0
            )
            hidden_grad = (back * slope).astype(BF)
            term = contract(hidden_grad, x, 0, 0)
            if c == 0:
                acc[...] = term
            else:
                acc[...] += term
            sums[here, :] = jnp.dot(spread, hidden, preferred_element_type=F32).astype(BF)
            c += 1
    copies[4].wait()
    grad_in_ref[...] = acc[...].T
    grad_out_ref[...] = contract(sums[...], cot_ref[...], 0, 0)


def expert_grads(pieces, first, back_hi, back_lo, gates, cot):
    width, hidden = first.shape
    vmem = pl.BlockSpec(memory_space=pltpu.VMEM)
    rest = (first, back_hi, back_lo, gates, cot)
    return pl.pallas_call(
        expert_kernel,
        out_shape=(
            jax.ShapeDtypeStruct((width, hidden), F32),
            jax.ShapeDtypeStruct((hidden, width), F32),
        ),
        in_specs=[pl.BlockSpec(memory_space=pltpu.HBM)] * (len(pieces) + 5),
        out_specs=(vmem, vmem),
        scratch_shapes=[
            *(pltpu.VMEM(r.shape, BF) for r in rest),
            pltpu.VMEM((hidden, width), F32),
            pltpu.VMEM((cot.shape[0], hidden), BF),
            pltpu.VMEM((sum(p.shape[0] for p in pieces), width), BF),
            pltpu.SemaphoreType.DMA((len(pieces) + 5,)),
        ],
        compiler_params=pltpu.CompilerParams(vmem_limit_bytes=60 * 1024 * 1024),
        cost_estimate=pl.CostEstimate(
            flops=5_000_000_000, bytes_accessed=13_000_000, transcendentals=1_000_000
        ),
    )(*pieces, *rest)


def slots(chosen, n_exp, capacity):
    n_tok = chosen.shape[0]
    onehot = (chosen[:, None] == jnp.arange(n_exp, dtype=jnp.int32)[None, :]).astype(BF)
    lower = (jnp.arange(n_tok)[:, None] > jnp.arange(n_tok)[None, :]).astype(BF)
    before = jnp.dot(lower, onehot, preferred_element_type=F32)
    rank = jnp.sum(before * onehot.astype(F32), axis=1).astype(jnp.int32)
    position = chosen * capacity + rank
    return (position[:, None] == jnp.arange(n_exp * capacity, dtype=jnp.int32)[None, :]).astype(BF)


def body(tokens, expert_id, gate_prob, w_in, w_out, head, image_cache, text_cache, pair_label):
    n_tok, width = tokens.shape
    n_exp = lax.axis_size("expert")
    n_dp = lax.axis_size("dp")
    capacity = 2 * n_tok // n_exp
    n_slots = n_exp * capacity
    n_pairs, wide = image_cache.shape
    row = lax.axis_index("dp")
    z_hi, x = row // SIDE, row % SIDE
    first = w_in[0]
    second = w_out[0]

    chosen = expert_id[:, :1]

    dispatch = slots(chosen[:, 0], n_exp, capacity)
    buffer = contract(dispatch, tokens, 0, 0).astype(BF).reshape(n_exp, capacity, width)
    own = lax.all_to_all(buffer, "expert", split_axis=0, concat_axis=0, tiled=True)
    own = own.reshape(n_slots, width)

    label_parts = jnp.stack([pair_label // 64, pair_label % 64], axis=1).astype(BF)
    slot_gate = jnp.dot(gate_prob[None, :], dispatch, preferred_element_type=F32).astype(BF)
    meta = jnp.concatenate([slot_gate, label_parts[:1], jnp.zeros((1, wide - n_slots - 2), BF)], axis=1)
    known = jnp.concatenate([text_cache, image_cache[:1], meta, jnp.zeros((6, wide), BF)], axis=0)
    known = jnp.stack(spread_along(known, "z_hi"))
    cuts = (0, n_pairs, n_pairs + 1, n_pairs + 2)
    known = [known[:, i:j].reshape(-1, wide) for i, j in zip(cuts, cuts[1:])]
    known = jnp.concatenate(known, axis=0)
    own = after(own, known)
    got = jnp.stack(spread_along(known, "z_lo"))
    cuts = tuple(SIDE * c for c in cuts)
    known = [got[:, i:j].reshape(-1, wide) for i, j in zip(cuts, cuts[1:])]
    known = jnp.concatenate(known, axis=0)

    later = after(own, known)
    below, above = shift(later, "z_hi", 1), shift(later, "z_hi", -1)
    known = spread_along(known, "x")
    near = [spread_along(jnp.concatenate(known[i : i + 2], axis=0), "y") for i in (0, 2)]
    near = [half for pair in zip(*near) for half in pair]

    own_x = gather_x(own)
    half = n_slots // 2
    far = jnp.concatenate([shift(below[:half], "z_hi", 1), shift(above[half:], "z_hi", -1)], axis=0)
    both = after(jnp.concatenate([below, above], axis=0), *near[2:7])
    left, right = shift(both, "x", 1), shift(both, "x", -1)
    other = [shift(jnp.concatenate(near[i : i + 2], axis=0), "core", 1) for i in range(0, 2 * SIDE, 2)]
    left_far = shift(after(left[:n_slots], far, *other), "x", 1)
    right_far = shift(after(right[n_slots:], far, *other), "x", -1)
    far_x = gather_x(after(far, left, right))
    pieces = [own_x, both, left, right, left_far, right_far, far_x]

    places = [(0, j, 0) for j in range(SIDE)]
    places += [(i, j, 1) for j in (0, -1, 1, 2) for i in (-1, 1)]
    places += [(2, j, 0) for j in range(SIDE)]
    along_z, along_x, moved = (jnp.asarray(c, jnp.int32) for c in np.asarray(places).T)
    order = (z_hi + along_z) % SIDE * SIDE + (x * moved + along_x) % SIDE
    want = (order[:, None] * n_exp + jnp.arange(n_exp, dtype=jnp.int32)[None, :]).reshape(-1, 1)
    own_meta = jnp.pad(label_parts.astype(F32), ((0, 0), (8, 118)))

    grad_image, cot, back_hi, back_lo, gates = image_grads(
        [after(near[0], left, right)] + near[1:] + other, want, image_cache, own_meta, head, second
    )
    grad_in, grad_out = expert_grads(pieces, first, back_hi, back_lo, gates, cot)
    return (grad_image, grad_in[None], grad_out[None])


def solution(mesh):
    placed = (
        P(("dp", "expert"), None),
        P(("dp", "expert"), None),
        P(("dp", "expert")),
        P("expert", None, "dp"),
        P("expert", "dp", None),
        P(),
        P(("dp", "expert"), None),
        P(("dp", "expert"), None),
        P(("dp", "expert")),
    )
    return jax.shard_map(
        body,
        mesh=mesh,
        in_specs=placed,
        out_specs=(P(("dp", "expert"), None), P("expert", None, "dp"), P("expert", "dp", None)),
        check_vma=False,
    )
```

```python
import jax
import jax.numpy as jnp
import numpy as np
from jax import lax
from jax.experimental import pallas as pl
from jax.experimental.pallas import tpu as pltpu
from jax.sharding import PartitionSpec as P

LOGIT_SCALE = 0.125
GELU_K = 0.7978845608
GELU_C = 0.044715
SIDE = 4
SIDES = {
    "z_hi": ("dp", (SIDE, SIDE), 0),
    "x": ("dp", (SIDE, SIDE), 1),
    "y": ("expert", (SIDE, SIDE, 2), 0),
    "z_lo": ("expert", (SIDE, SIDE, 2), 1),
    "core": ("expert", (SIDE, SIDE, 2), 2),
}
BF = jnp.bfloat16
F32 = jnp.float32


def contract(a, b, da, db):
    return lax.dot_general(a, b, (((da,), (db,)), ((), ())), preferred_element_type=F32)


def gelu_parts(pre):
    inner = GELU_K * (pre + GELU_C * pre * pre * pre)
    tangent = jnp.tanh(inner)
    value = 0.5 * pre * (1.0 + tangent)
    slope = 0.5 * (1.0 + tangent) + 0.5 * pre * (1.0 - tangent * tangent) * GELU_K * (
        1.0 + 3.0 * GELU_C * pre * pre
    )
    return (value, slope)


def shift(a, axis, by):
    name, sizes, side = SIDES[axis]
    ring = []
    for at in np.ndindex(*sizes):
        to = list(at)
        to[side] = (to[side] + by) % sizes[side]
        ring.append((int(np.ravel_multi_index(at, sizes)), int(np.ravel_multi_index(to, sizes))))
    return lax.ppermute(a, name, ring)


def spread_along(a, axis):
    name, sizes, side = SIDES[axis]
    return [a] + [shift(a, axis, k) for k in range(1, sizes[side])]


def gather_x(a):
    rows = [[z * SIDE + x for x in range(SIDE)] for z in range(SIDE)]
    return lax.all_gather(a, "dp", axis=0, tiled=True, axis_index_groups=rows)


def after(a, *others):
    return lax.optimization_barrier((a, *others))[0]


def loss_kernel(*refs):
    n = 4 * SIDE // 2
    halves, wholes, refs = refs[:n], refs[n : n + n // 2], refs[n + n // 2 :]
    want_ref, image_ref, own_meta_ref, head_ref, second_ref = refs[:5]
    grad_image_ref, cot_ref, back_hi_ref, back_lo_ref, gate_ref = refs[5:10]
    images, reps, metas, logit, weights, hits = refs[10:]
    n_rep = want_ref.shape[0]
    n_own = image_ref.shape[0]
    n_all = images.shape[0]
    each = n_rep // n // SIDE
    step = n_own * each * SIDE
    block = (n_own + 2) * each
    row, expert = lax.axis_index("dp"), lax.axis_index("expert")
    z_hi, x = row >> 2, row & 3
    y, z_lo, core = expert >> 3, expert >> 1 & 3, expert & 1

    def device(part, k):
        at = ((z_hi - (k & 3)) & 3) * 4 + ((x - (k >> 4)) & 3)
        at = (at * 4 + ((y - part % SIDE) & 3)) * 4 + ((z_lo - (k >> 2 & 3)) & 3)
        return at * 2 + ((core - part // SIDE) & 1)

    def counted(size):
        return lax.broadcasted_iota(jnp.int32, (1, size), 1)

    def piece(p, q, offset, size):
        if p < n // 2:
            return halves[2 * p + q // 2][pl.ds(q % 2 * block + offset, size), :]
        return wholes[p - n // 2][pl.ds(q * block + offset, size), :]

    def gathered(offset):
        for p in range(n):
            for q in range(SIDE):
                reps[pl.ds((p * SIDE + q) * each, each), :] = piece(p, q, offset, each)
        return reps[...]

    def captions(p):
        return jnp.concatenate([piece(p, q, 0, n_own * each) for q in range(SIDE)], axis=0)

    sources = jnp.concatenate([device(p, counted(SIDE * each)) for p in range(n)], axis=1)
    pick = (want_ref[...] == sources).astype(BF)
    images[:n_rep, :] = jnp.dot(pick, gathered(n_own * each), preferred_element_type=F32).astype(BF)
    images[n_rep:, :] = jnp.zeros((n_all - n_rep, images.shape[1]), BF)
    images[n_rep : n_rep + n_own, :] = image_ref[...]
    found = jnp.dot(pick, gathered((n_own + 1) * each), preferred_element_type=F32)
    width = found.shape[1]
    source = lax.broadcasted_iota(jnp.int32, (width, 128), 0)
    slot = lax.broadcasted_iota(jnp.int32, (width, 128), 1)
    label_at = 256
    select = jnp.where(slot < 8, expert * 8 + slot, label_at + slot - 8)
    select = ((source == select) & (slot < 10)).astype(BF)
    found = jnp.dot(found.astype(BF), select, preferred_element_type=F32)
    gate_ref[...] = found.astype(BF)
    metas[:n_rep, :] = found
    metas[n_rep:, :] = jnp.full((n_all - n_rep, 128), -8.0, F32)
    metas[n_rep : n_rep + n_own, :] = own_meta_ref[...]
    labels = (metas[:, 8:9] * 64.0 + metas[:, 9:10]).astype(jnp.int32)
    top = None
    for p in range(n):
        ids = device(p, counted(step) >> 3) * 8 + (counted(step) & 7)
        part = LOGIT_SCALE * contract(images[...], captions(p), 1, 1)
        logit[:, pl.ds(p * step, step)] = part
        hits[:, pl.ds(p * step, step)] = (labels == ids).astype(BF)
        peak = jnp.max(part, axis=1, keepdims=True)
        top = peak if top is None else jnp.maximum(top, peak)
    total = jnp.zeros((n_all, 1), F32)
    for p in range(n):
        expo = jnp.exp(logit[:, pl.ds(p * step, step)] - top)
        total = total + jnp.sum(expo, axis=1, keepdims=True)
        weights[:, pl.ds(p * step, step)] = expo.astype(BF)
    mix, labelled = jnp.zeros(images.shape, F32), jnp.zeros(images.shape, F32)
    for p in range(n):
        rows = captions(p)
        mix += jnp.dot(weights[:, pl.ds(p * step, step)], rows, preferred_element_type=F32)
        labelled += jnp.dot(hits[:, pl.ds(p * step, step)], rows, preferred_element_type=F32)
    grad = LOGIT_SCALE * (mix / total - labelled)
    grad_image_ref[...] = grad[n_rep : n_rep + n_own, :]
    cot = contract(grad[:n_rep].astype(BF), head_ref[...], 1, 1).astype(BF)
    cot_ref[...] = cot
    back = contract(cot, second_ref[...], 1, 1)
    back_hi = back.astype(BF)
    back_hi_ref[...] = back_hi
    back_lo_ref[...] = (back - back_hi.astype(F32)).astype(BF)


def image_grads(parts, want, image_cache, own_meta, head, second):
    n_rep, n_own, wide = want.shape[0], image_cache.shape[0], image_cache.shape[1]
    n_all = n_rep + 16
    n_text = n_rep * n_own
    hidden, width = second.shape
    vmem = pl.BlockSpec(memory_space=pltpu.VMEM)
    return pl.pallas_call(
        loss_kernel,
        out_shape=(
            jax.ShapeDtypeStruct((n_own, wide), F32),
            jax.ShapeDtypeStruct((n_rep, width), BF),
            jax.ShapeDtypeStruct((n_rep, hidden), BF),
            jax.ShapeDtypeStruct((n_rep, hidden), BF),
            jax.ShapeDtypeStruct((n_rep, 128), BF),
        ),
        in_specs=[vmem] * (len(parts) + 5),
        out_specs=(vmem,) * 5,
        scratch_shapes=[
            pltpu.VMEM((n_all, wide), BF),
            pltpu.VMEM((n_rep, wide), BF),
            pltpu.VMEM((n_all, 128), F32),
            pltpu.VMEM((n_all, n_text), F32),
            pltpu.VMEM((n_all, n_text), BF),
            pltpu.VMEM((n_all, n_text), BF),
        ],
        compiler_params=pltpu.CompilerParams(vmem_limit_bytes=60 * 1024 * 1024),
        cost_estimate=pl.CostEstimate(
            flops=10_000_000_000, bytes_accessed=9_000_000, transcendentals=3_000_000
        ),
    )(*parts, want, image_cache, own_meta, head, second)


def expert_kernel(*refs):
    n = len(refs) - 16
    sources, targets = refs[: n + 5], refs[n + 7 : n + 12]
    grad_in_ref, grad_out_ref = refs[n + 5 : n + 7]
    acc, sums, held = refs[n + 12 : n + 15]
    sems = refs[n + 15]
    first_ref, back_hi_ref, back_lo_ref, gate_ref, cot_ref = targets
    copies, at = [], 0
    for i in range(5):
        copies.append(pltpu.make_async_copy(sources[n + i], targets[i], sems.at[n + i]))
    for i in range(n):
        size = sources[i].shape[0]
        copies.append(pltpu.make_async_copy(sources[i], held.at[pl.ds(at, size)], sems.at[i]))
        at += size
    for copy in copies[:4] + copies[5:] + copies[4:5]:
        copy.start()
    for copy in copies[:4]:
        copy.wait()
    images = 32
    per = 8
    rows = images * per
    first = first_ref[...]
    column = lax.broadcasted_iota(jnp.int32, (images, rows), 1)
    mask = column // per == lax.broadcasted_iota(jnp.int32, (images, rows), 0)
    widen = (
        lax.broadcasted_iota(jnp.int32, (128, rows), 1) % per
        == lax.broadcasted_iota(jnp.int32, (128, rows), 0)
    ).astype(BF)
    c = 0
    for i in range(n):
        copies[5 + i].wait()
        for _ in range(sources[i].shape[0] // rows):
            here = pl.ds(c * images, images)
            x = held[pl.ds(c * rows, rows), :]
            gates = jnp.dot(gate_ref[here, :], widen, preferred_element_type=F32)
            spread = jnp.where(mask, gates, 0.0).astype(BF)
            pre = jnp.dot(x, first, preferred_element_type=F32)
            value, slope = gelu_parts(pre)
            hidden = value.astype(BF)
            back = contract(spread, back_hi_ref[here, :], 0, 0) + contract(
                spread, back_lo_ref[here, :], 0, 0
            )
            hidden_grad = (back * slope).astype(BF)
            term = contract(hidden_grad, x, 0, 0)
            if c == 0:
                acc[...] = term
            else:
                acc[...] += term
            sums[here, :] = jnp.dot(spread, hidden, preferred_element_type=F32).astype(BF)
            c += 1
    copies[4].wait()
    grad_in_ref[...] = acc[...].T
    grad_out_ref[...] = contract(sums[...], cot_ref[...], 0, 0)


def expert_grads(pieces, first, back_hi, back_lo, gates, cot):
    width, hidden = first.shape
    vmem = pl.BlockSpec(memory_space=pltpu.VMEM)
    rest = (first, back_hi, back_lo, gates, cot)
    return pl.pallas_call(
        expert_kernel,
        out_shape=(
            jax.ShapeDtypeStruct((width, hidden), F32),
            jax.ShapeDtypeStruct((hidden, width), F32),
        ),
        in_specs=[pl.BlockSpec(memory_space=pltpu.HBM)] * (len(pieces) + 5),
        out_specs=(vmem, vmem),
        scratch_shapes=[
            *(pltpu.VMEM(r.shape, BF) for r in rest),
            pltpu.VMEM((hidden, width), F32),
            pltpu.VMEM((cot.shape[0], hidden), BF),
            pltpu.VMEM((sum(p.shape[0] for p in pieces), width), BF),
            pltpu.SemaphoreType.DMA((len(pieces) + 5,)),
        ],
        compiler_params=pltpu.CompilerParams(vmem_limit_bytes=60 * 1024 * 1024),
        cost_estimate=pl.CostEstimate(
            flops=5_000_000_000, bytes_accessed=13_000_000, transcendentals=1_000_000
        ),
    )(*pieces, *rest)


def slots(chosen, n_exp, capacity):
    n_tok = chosen.shape[0]
    onehot = (chosen[:, None] == jnp.arange(n_exp, dtype=jnp.int32)[None, :]).astype(BF)
    lower = (jnp.arange(n_tok)[:, None] > jnp.arange(n_tok)[None, :]).astype(BF)
    before = jnp.dot(lower, onehot, preferred_element_type=F32)
    rank = jnp.sum(before * onehot.astype(F32), axis=1).astype(jnp.int32)
    position = chosen * capacity + rank
    return (position[:, None] == jnp.arange(n_exp * capacity, dtype=jnp.int32)[None, :]).astype(BF)


def body(tokens, expert_id, gate_prob, w_in, w_out, head, image_cache, text_cache, pair_label):
    n_tok, width = tokens.shape
    n_exp = lax.axis_size("expert")
    n_dp = lax.axis_size("dp")
    capacity = 2 * n_tok // n_exp
    n_slots = n_exp * capacity
    n_pairs, wide = image_cache.shape
    row = lax.axis_index("dp")
    z_hi, x = row // SIDE, row % SIDE
    first = w_in[0]
    second = w_out[0]

    chosen = expert_id[:, :1]

    dispatch = slots(chosen[:, 0], n_exp, capacity)
    buffer = contract(dispatch, tokens, 0, 0).astype(BF).reshape(n_exp, capacity, width)
    own = lax.all_to_all(buffer, "expert", split_axis=0, concat_axis=0, tiled=True)
    own = own.reshape(n_slots, width)

    label_parts = jnp.stack([pair_label // 64, pair_label % 64], axis=1).astype(BF)
    slot_gate = jnp.dot(gate_prob[None, :], dispatch, preferred_element_type=F32).astype(BF)
    meta = jnp.concatenate([slot_gate, label_parts[:1], jnp.zeros((1, wide - n_slots - 2), BF)], axis=1)
    known = jnp.concatenate([text_cache, image_cache[:1], meta, jnp.zeros((6, wide), BF)], axis=0)
    known = jnp.stack(spread_along(known, "z_hi"))
    cuts = (0, n_pairs, n_pairs + 1, n_pairs + 2)
    known = [known[:, i:j].reshape(-1, wide) for i, j in zip(cuts, cuts[1:])]
    known = jnp.concatenate(known, axis=0)
    own = after(own, known)
    got = jnp.stack(spread_along(known, "z_lo"))
    cuts = tuple(SIDE * c for c in cuts)
    known = [got[:, i:j].reshape(-1, wide) for i, j in zip(cuts, cuts[1:])]
    known = jnp.concatenate(known, axis=0)

    later = after(own, known)
    below, above = shift(later, "z_hi", 1), shift(later, "z_hi", -1)
    known = spread_along(known, "x")
    near = [spread_along(jnp.concatenate(known[i : i + 2], axis=0), "y") for i in (0, 2)]
    near = [half for pair in zip(*near) for half in pair]

    own_x = gather_x(own)
    half = n_slots // 2
    far = jnp.concatenate([shift(below[:half], "z_hi", 1), shift(above[half:], "z_hi", -1)], axis=0)
    both = after(jnp.concatenate([below, above], axis=0), *near[2:5])
    left, right = shift(both, "x", 1), shift(both, "x", -1)
    other = [shift(jnp.concatenate(near[i : i + 2], axis=0), "core", 1) for i in range(0, 2 * SIDE, 2)]
    left_far = shift(after(left[:n_slots], far, *other), "x", 1)
    right_far = shift(after(right[n_slots:], far, *other), "x", -1)
    far_x = gather_x(after(far, left, right))
    pieces = [own_x, both, left, right, left_far, right_far, far_x]

    places = [(0, j, 0) for j in range(SIDE)]
    places += [(i, j, 1) for j in (0, -1, 1, 2) for i in (-1, 1)]
    places += [(2, j, 0) for j in range(SIDE)]
    along_z, along_x, moved = (jnp.asarray(c, jnp.int32) for c in np.asarray(places).T)
    order = (z_hi + along_z) % SIDE * SIDE + (x * moved + along_x) % SIDE
    want = (order[:, None] * n_exp + jnp.arange(n_exp, dtype=jnp.int32)[None, :]).reshape(-1, 1)
    own_meta = jnp.pad(label_parts.astype(F32), ((0, 0), (8, 118)))

    grad_image, cot, back_hi, back_lo, gates = image_grads(
        [after(near[0], left, right)] + near[1:] + other, want, image_cache, own_meta, head, second
    )
    grad_in, grad_out = expert_grads(pieces, first, back_hi, back_lo, gates, cot)
    return (grad_image, grad_in[None], grad_out[None])


def solution(mesh):
    placed = (
        P(("dp", "expert"), None),
        P(("dp", "expert"), None),
        P(("dp", "expert")),
        P("expert", None, "dp"),
        P("expert", "dp", None),
        P(),
        P(("dp", "expert"), None),
        P(("dp", "expert"), None),
        P(("dp", "expert")),
    )
    return jax.shard_map(
        body,
        mesh=mesh,
        in_specs=placed,
        out_specs=(P(("dp", "expert"), None), P("expert", None, "dp"), P("expert", "dp", None)),
        check_vma=False,
    )
```
